256 devices in a mesh: blk: 32 (over z, y_hi, core), grp: 8 (over y_lo, x).
Axes of the slice: x: 4, y: 4 (y_hi: 2, y_lo: 2; y = y_hi * 2 + y_lo), z: 8, core: 2. Of those that a mesh axis runs over, the one named last changes fastest.
Arguments:
- image_vectors: bfloat16 [196608, 1152], P(('blk', 'grp')), may hold values from -12 to 12, as said below
- caption_vectors: bfloat16 [196608, 1152], P(('blk', 'grp')), may hold values from -12 to 12, as said below
- caption_labels: int32 [196608], P(('blk', 'grp')), may hold values from 0 to 196607
- log_logit_scale: float32 [1], replicated, may hold values from 1.6 to 2.4
- logit_offset_bias: float32 [1], replicated, may hold values from -6 to -2
Outputs:
- grad_image: float32 [196608, 1152], P(('blk', 'grp'))
- grad_text: float32 [196608, 1152], P(('blk', 'grp'))
The draws below stay inside these ranges and needn't reach their ends.
Inputs may be any that keep to these rules, and one draw needn't show every extreme that they name: `image_vectors`: entries of order one. `caption_vectors`: entries of order one.
All inputs are finite; a program needn't handle non-finite values.
Results may differ from the reference program's by a relative error of at most 0.0035.
Values may be sent and summed in bfloat16 or wider, within the bound.
A program may use at most 128 MiB of HBM per device.

```python
import math
import jax
import jax.numpy as jnp
import numpy as np
from jax import lax

D = 1152
ROWS_DEV = 768
TOKENS = 196608
N_BLK = 32
N_GRP = 8


def shared_base(key, centre_weight):
    cluster_key = jax.random.fold_in(key, 101)
    centre_key = jax.random.fold_in(key, 103)
    row_key = jax.random.fold_in(key, 107)
    membership = jax.random.randint(cluster_key, (TOKENS,), 0, 64)
    centres = jax.random.normal(centre_key, (64, D), jnp.float32)
    row_noise = jax.random.normal(row_key, (TOKENS, D), jnp.float32)
    return centre_weight * jnp.take(centres, membership, axis=0) + 0.6 * row_noise


def draw_image_vectors(key, part):
    base = shared_base(key, 0.8)
    key = jax.random.fold_in(key, 11)
    noise = jax.random.normal(key, (TOKENS, D), jnp.float32)
    scales = jnp.exp(jax.random.uniform(jax.random.fold_in(key, 5), (TOKENS, 1), jnp.float32, -1.0, 1.0))
    return jnp.clip((base + 0.6 * noise) * scales, -12.0, 12.0).astype(jnp.bfloat16)


def draw_caption_vectors(key, part):
    base = shared_base(key, 0.8)
    key = jax.random.fold_in(key, 23)
    noise = jax.random.normal(key, (TOKENS, D), jnp.float32)
    scales = jnp.exp(jax.random.uniform(jax.random.fold_in(key, 7), (TOKENS, 1), jnp.float32, -1.0, 1.0))
    return jnp.clip((base + 0.6 * noise) * scales, -12.0, 12.0).astype(jnp.bfloat16)


def touch_ends(values, stream_key, smallest, largest):
    dims = values.shape
    place = [jax.random.randint(jax.random.fold_in(stream_key, axis), (), 0, dims[axis]) for axis in range(len(dims))]
    values = values.at[tuple(place)].set(smallest)
    longest = dims.index(max(dims))
    place[longest] = (place[longest] + 1) % dims[longest]
    return values.at[tuple(place)].set(largest)


def wide_ids(own_key, shape, number_of, slope):
    loads = [min(1 << octave, number_of + 1 - (1 << octave)) * (1 << 20) // math.isqrt((1 << octave) ** slope) + 1 for octave in range((number_of + 1).bit_length()) if 1 << octave <= number_of]
    deviation = 1 + sum(loads) // (1 << 30)
    listing = np.cumsum(np.array([max(1, weight // deviation) for weight in loads]))
    ticket = jax.random.randint(jax.random.fold_in(own_key, 1), shape, 0, int(listing[len(loads) - 1]))
    start = jnp.left_shift(1, jnp.searchsorted(jnp.asarray(listing, jnp.int32), ticket, side="right").astype(jnp.int32))
    grade = start - 1 + jax.random.randint(jax.random.fold_in(own_key, 4), shape, 0, 1 << 30) % jnp.minimum(start, number_of + 1 - start)
    return jax.random.permutation(jax.random.fold_in(own_key, 2), number_of)[grade].astype(jnp.int32)


def setup_inputs(seed: int = 0) -> dict:
    seeds = jax.random.split(jax.random.key(seed), 6)
    image_vectors = draw_image_vectors(jax.random.fold_in(seeds[5], 71), 0)
    caption_vectors = draw_caption_vectors(jax.random.fold_in(seeds[5], 71), 0)
    caption_labels = touch_ends(wide_ids(seeds[2], (TOKENS,), TOKENS, 2), jax.random.fold_in(seeds[2], 3), 0, TOKENS - 1).astype(jnp.int32)
    log_logit_scale = jnp.clip(jax.random.uniform(seeds[3], (1,), jnp.float32, 1.6, 2.4), 1.6, 2.4)
    logit_offset_bias = jnp.clip(jax.random.uniform(seeds[4], (1,), jnp.float32, -6.0, -2.0), -6.0, -2.0)
    return dict(image_vectors=image_vectors, caption_vectors=caption_vectors, caption_labels=caption_labels, log_logit_scale=log_logit_scale, logit_offset_bias=logit_offset_bias)


def normalize(embedding):
    values = embedding.astype(jnp.float32)
    inverse = lax.rsqrt(lax.optimization_barrier(jnp.sum(values * values, axis=-1, keepdims=True)) + 1e-06)
    return (values * inverse, inverse)

def pairwise_gradient(image_lower, text_lower, image_labels, text_labels, logit_scale, shifted_bias):
    pair_logits = logit_scale * jnp.dot(image_lower, text_lower.T, preferred_element_type=jnp.float32) + shifted_bias
    positive_mask = (image_labels[:, None] == text_labels[None, :]).astype(jnp.float32)
    weight_tile_matrix = ((jax.nn.sigmoid(pair_logits) - positive_mask) * logit_scale).astype(jnp.bfloat16)
    image_part = jnp.dot(weight_tile_matrix, text_lower, preferred_element_type=jnp.float32)
    text_part = jnp.dot(weight_tile_matrix.T, image_lower, preferred_element_type=jnp.float32)
    return (image_part, text_part)

def partner_blocks(array, width):
    lead = array.shape[2:]
    folded = array.reshape((N_BLK, N_GRP // 2, 2) + lead)
    return folded[:, :, ::-1].reshape((N_BLK, N_GRP) + lead)

def reference(image_vectors, caption_vectors, caption_labels, log_logit_scale, logit_offset_bias):
    logit_scale = jnp.exp(log_logit_scale[0])
    shifted_bias = logit_offset_bias[0]
    image_dir, image_inv = normalize(image_vectors)
    text_dir, text_inv = normalize(caption_vectors)
    image_lower = image_dir.astype(jnp.bfloat16)
    text_lower = text_dir.astype(jnp.bfloat16)
    block_shape = (N_BLK, N_GRP, ROWS_DEV, D)
    images4 = image_lower.reshape(block_shape)
    texts4 = text_lower.reshape(block_shape)
    labels3 = caption_labels.reshape((N_BLK, N_GRP, ROWS_DEV))
    texts_left = jnp.roll(texts4, 1, axis=0)
    neighbour_labels = jnp.roll(labels3, 1, axis=0)
    texts_partner = partner_blocks(texts4, D)
    companion_labels = partner_blocks(labels3, 1)
    count = N_BLK * N_GRP

    def flat(array):
        return array.reshape((count,) + array.shape[2:])

    def block_grads(block):
        image_block_rows, text_block_rows, neighbour_block, companion_block, label_block_rows, label_neighbour, label_companion = block
        local_image, local_text = pairwise_gradient(image_block_rows, text_block_rows, label_block_rows, label_block_rows, logit_scale, shifted_bias)
        neighbour_image, neighbour_text = pairwise_gradient(image_block_rows, neighbour_block, label_block_rows, label_neighbour, logit_scale, shifted_bias)
        companion_image, companion_text = pairwise_gradient(image_block_rows, companion_block, label_block_rows, label_companion, logit_scale, shifted_bias)
        return (local_image + neighbour_image + companion_image, local_text, neighbour_text, companion_text)
    grad_image_dir, local_text, neighbour_text, companion_text = lax.map(block_grads, (flat(images4), flat(texts4), flat(texts_left), flat(texts_partner), flat(labels3), flat(neighbour_labels), flat(companion_labels)))
    neighbour_text = jnp.roll(neighbour_text.reshape(block_shape), -1, axis=0)
    companion_text = partner_blocks(companion_text.reshape(block_shape), D)
    grad_text_dir = (local_text.reshape(block_shape) + neighbour_text + companion_text).reshape((N_BLK * N_GRP * ROWS_DEV, D))
    grad_image_dir = grad_image_dir.reshape((N_BLK * N_GRP * ROWS_DEV, D))
    grad_image = image_inv * (grad_image_dir - image_dir * lax.optimization_barrier(jnp.sum(image_dir * grad_image_dir, axis=-1, keepdims=True)))
    grad_text = text_inv * (grad_text_dir - text_dir * lax.optimization_barrier(jnp.sum(text_dir * grad_text_dir, axis=-1, keepdims=True)))
    return (grad_image, grad_text)
```

```python
import jax
import jax.numpy as jnp
from jax import lax
from jax.experimental import pallas as pl
from jax.experimental.pallas import tpu as pltpu
from jax.sharding import PartitionSpec as P

ROWS = 768
WIDTH = 1152
STEP = 256
STEPS = ROWS // STEP
PIECE = 128
PIECES = ROWS // PIECE
LANES = 128
MESH = pl.DeviceIdType.MESH


def rows_of(index, size):
    return pl.ds(pl.multiple_of(index * size, size), size)


def normalize_rows(source, rows, low, low_rows, inverse=None):
    values = source[rows, :].astype(jnp.float32)
    scaled = lax.rsqrt(jnp.sum(values * values, axis=-1, keepdims=True) + 1e-06)
    low[low_rows, :] = (values * scaled).astype(jnp.bfloat16)
    if inverse is not None:
        inverse[rows, :] = scaled


def kernel(
    image_hbm,
    caption_hbm,
    labels_hbm,
    log_scale,
    offset,
    grad_image,
    grad_text,
    image,
    caption,
    labels,
    image_low,
    text_low,
    image_inv,
    text_inv,
    label_column,
    left_labels,
    partner_labels,
    left_text,
    partner_text,
    low,
    part,
    left_out,
    partner_out,
    left_in,
    partner_in,
    local_sems,
    label_send,
    label_recv,
    left_send,
    left_recv,
    partner_send,
    partner_recv,
    left_back_send,
    left_back_recv,
    partner_back_send,
    partner_back_recv,
):
    blk, grp = lax.axis_index("blk"), lax.axis_index("grp")
    count = lax.axis_size("blk")
    right = (lax.rem(blk + 1, count), grp)
    left = (lax.rem(blk + count - 1, count), grp)
    partner = (blk, grp + 1 - 2 * lax.rem(grp, 2))

    loads = [
        pltpu.make_async_copy(source, target, local_sems.at[i])
        for i, (source, target) in enumerate(((labels_hbm, labels), (image_hbm, image), (caption_hbm, caption)))
    ]
    for load in loads:
        load.start()

    barrier = pltpu.get_barrier_semaphore()
    for other in (partner, right, left):
        pl.semaphore_signal(barrier, inc=1, device_id=other, device_id_type=MESH)
    pl.semaphore_wait(barrier, 3)

    def remote(source, target, send, recv, device):
        return pltpu.make_async_remote_copy(source, target, send, recv, device_id=device, device_id_type=MESH)

    def text_copy(target, send, recv, device, i):
        rows = rows_of(i, STEP)
        return remote(caption_hbm.at[rows, :], target.at[rows, :], send.at[i], recv.at[i], device)

    to_partner = [text_copy(partner_text, partner_send, partner_recv, partner, i) for i in range(STEPS)]
    to_right = [text_copy(left_text, left_send, left_recv, right, i) for i in range(STEPS)]
    label_copies = [
        remote(labels_hbm, partner_labels, label_send.at[0], label_recv.at[0], partner),
        remote(labels_hbm, left_labels, label_send.at[1], label_recv.at[1], right),
    ]
    for copy in label_copies:
        copy.start()
    for a, b in zip(to_partner, to_right):
        a.start()
        b.start()

    def left_back(i):
        rows = rows_of(i, STEP)
        return remote(left_out.at[rows, :], left_in.at[rows, :], left_back_send.at[i], left_back_recv.at[i], left)

    def partner_back(i):
        rows = rows_of(i, PIECE)
        return remote(
            partner_out.at[rows, :], partner_in.at[rows, :], partner_back_send.at[i], partner_back_recv.at[i], partner
        )

    scale = jnp.exp(jnp.full((1, STEP), log_scale[0], jnp.float32))
    bias = offset[0]

    loads[0].wait()
    for i in range(ROWS // LANES):
        label_column[i * LANES : (i + 1) * LANES, :] = jnp.broadcast_to(labels[i : i + 1, :], (LANES, LANES)).T

    loads[1].wait()

    @pl.loop(0, PIECES)
    def _(i):
        rows = rows_of(i, PIECE)
        normalize_rows(image, rows, image_low, rows, image_inv)

    loads[2].wait()

    @pl.loop(0, PIECES)
    def _(i):
        rows = rows_of(i, PIECE)
        normalize_rows(caption, rows, text_low, rows, text_inv)

    def tile(step, text, text_rows, text_labels, first):
        per = STEP // LANES
        row = jnp.concatenate([text_labels[pl.ds(step * per + j, 1), :] for j in range(per)], axis=1)

        @pl.loop(0, ROWS // STEP)
        def _(m):
            rows = rows_of(m, STEP)
            images = image_low[rows, :]
            texts = text[text_rows, :]
            products = lax.dot_general(images, texts, (((1,), (1,)), ((), ())), preferred_element_type=jnp.float32)
            column = jnp.concatenate([label_column[rows, :]] * per, axis=1)
            positive = (column == row).astype(jnp.float32)
            weight = ((jax.nn.sigmoid(scale * products + bias) - positive) * scale).astype(jnp.bfloat16)
            update = jnp.dot(weight, texts, preferred_element_type=jnp.float32)

            @pl.when(jnp.logical_and(first, step == 0))
            def _():
                grad_image[rows, :] = update

            @pl.when(jnp.logical_not(jnp.logical_and(first, step == 0)))
            def _():
                grad_image[rows, :] += update

            back = lax.dot_general(weight, images, (((0,), (0,)), ((), ())), preferred_element_type=jnp.float32)

            @pl.when(m == 0)
            def _():
                part[...] = back

            @pl.when(m > 0)
            def _():
                part[...] += back

    @pl.loop(0, STEPS)
    def _(c):
        rows = rows_of(c, STEP)
        tile(c, text_low, rows, labels, True)
        grad_text[rows, :] = part[...]

    def normalize_arrived(text, c):
        @pl.loop(0, STEP // PIECE)
        def _(i):
            normalize_rows(text, rows_of(c * (STEP // PIECE) + i, PIECE), low, rows_of(i, PIECE))

    label_copies[1].wait()

    @pl.loop(0, STEPS)
    def _(c):
        text_copy(left_text, left_send, left_recv, right, c).wait_recv()
        normalize_arrived(left_text, c)
        tile(c, low, pl.ds(0, STEP), left_labels, False)
        left_out[rows_of(c, STEP), :] = part[...].astype(jnp.bfloat16)
        left_back(c).start()

    label_copies[0].wait()

    @pl.loop(0, STEPS)
    def _(c):
        text_copy(partner_text, partner_send, partner_recv, partner, c).wait_recv()
        normalize_arrived(partner_text, c)
        tile(c, low, pl.ds(0, STEP), partner_labels, False)
        partner_out[rows_of(c, STEP), :] = part[...].astype(jnp.bfloat16)
        for j in range(STEP // PIECE):
            partner_back(c * (STEP // PIECE) + j).start()

    def project_back(grad, source, inverse, rows, gradient):
        inv = inverse[rows, :]
        direction = source[rows, :].astype(jnp.float32) * inv
        along = jnp.sum(direction * gradient, axis=-1, keepdims=True)
        grad[rows, :] = inv * (gradient - direction * along)

    @pl.loop(0, PIECES)
    def _(i):
        rows = rows_of(i, PIECE)
        project_back(grad_image, image, image_inv, rows, grad_image[rows, :])

    @pl.loop(0, STEPS)
    def _(c):
        left_back(c).wait_recv()
        rows = rows_of(c, STEP)
        grad_text[rows, :] += left_in[rows, :].astype(jnp.float32)

    for c in range(STEPS):
        to_right[c].wait_send()
        to_partner[c].wait_send()
        left_back(c).wait_send()

    @pl.loop(0, PIECES)
    def _(i):
        partner_back(i).wait()
        rows = rows_of(i, PIECE)
        gradient = grad_text[rows, :] + partner_in[rows, :].astype(jnp.float32)
        project_back(grad_text, caption, text_inv, rows, gradient)


def local(image_vectors, caption_vectors, caption_labels, log_logit_scale, logit_offset_bias):
    block = (ROWS, WIDTH)
    label_block = (ROWS // LANES, LANES)
    hbm = pl.BlockSpec(memory_space=pltpu.HBM)
    smem = pl.BlockSpec(memory_space=pltpu.SMEM)
    vmem = pl.BlockSpec(memory_space=pltpu.VMEM)
    dma = pltpu.SemaphoreType.DMA
    low_block = pltpu.VMEM(block, jnp.bfloat16)
    return pl.pallas_call(
        kernel,
        out_shape=(pltpu.VMEM(block, jnp.float32), pltpu.VMEM(block, jnp.float32)),
        in_specs=[hbm, hbm, hbm, smem, smem],
        out_specs=(vmem, vmem),
        scratch_shapes=[
            low_block,
            low_block,
            pltpu.VMEM(label_block, jnp.int32),
            low_block,
            low_block,
            pltpu.VMEM((ROWS, 1), jnp.float32),
            pltpu.VMEM((ROWS, 1), jnp.float32),
            pltpu.VMEM((ROWS, LANES), jnp.int32),
            pltpu.VMEM(label_block, jnp.int32),
            pltpu.VMEM(label_block, jnp.int32),
            low_block,
            low_block,
            pltpu.VMEM((STEP, WIDTH), jnp.bfloat16),
            pltpu.VMEM((STEP, WIDTH), jnp.float32),
            low_block,
            low_block,
            low_block,
            low_block,
            dma((3,)),
            dma((2,)),
            dma((2,)),
            dma((STEPS,)),
            dma((STEPS,)),
            dma((STEPS,)),
            dma((STEPS,)),
            dma((STEPS,)),
            dma((STEPS,)),
            dma((PIECES,)),
            dma((PIECES,)),
        ],
        compiler_params=pltpu.CompilerParams(
            collective_id=0, has_side_effects=True, vmem_limit_bytes=32 * 1024 * 1024
        ),
        cost_estimate=pl.CostEstimate(
            flops=18 * ROWS * ROWS * WIDTH, bytes_accessed=12 * ROWS * WIDTH, transcendentals=3 * ROWS * ROWS
        ),
        name="contrast",
    )(
        pltpu.with_memory_space_constraint(image_vectors, pltpu.HBM),
        pltpu.with_memory_space_constraint(caption_vectors, pltpu.HBM),
        pltpu.with_memory_space_constraint(caption_labels.reshape(label_block), pltpu.HBM),
        log_logit_scale,
        logit_offset_bias,
    )


def solution(mesh):
    rows = P(("blk", "grp"), None)
    return jax.shard_map(
        local, mesh=mesh, in_specs=(rows, rows, P(("blk", "grp")), P(), P()), out_specs=(rows, rows), check_vma=False
    )
```

```python
import jax
import jax.numpy as jnp
from jax import lax
from jax.experimental import pallas as pl
from jax.experimental.pallas import tpu as pltpu
from jax.sharding import PartitionSpec as P

ROWS = 768
WIDTH = 1152
STEP = 256
STEPS = ROWS // STEP
PIECE = 128
PIECES = ROWS // PIECE
LANES = 128
WRITES = 1
MESH = pl.DeviceIdType.MESH


def rows_of(index, size):
    return pl.ds(pl.multiple_of(index * size, size), size)


def normalize_rows(source, rows, low, low_rows, inverse=None):
    values = source[rows, :].astype(jnp.float32)
    scaled = lax.rsqrt(jnp.sum(values * values, axis=-1, keepdims=True) + 1e-06)
    low[low_rows, :] = (values * scaled).astype(jnp.bfloat16)
    if inverse is not None:
        inverse[rows, :] = scaled


def kernel(
    image_hbm,
    caption_hbm,
    labels_hbm,
    log_scale,
    offset,
    grad_image,
    grad_text,
    image,
    caption,
    labels,
    image_low,
    text_low,
    image_inv,
    text_inv,
    label_column,
    left_labels,
    partner_labels,
    left_text,
    partner_text,
    low,
    part,
    left_out,
    partner_out,
    left_in,
    partner_in,
    local_sems,
    inside_sem,
    label_send,
    label_recv,
    left_send,
    left_recv,
    partner_send,
    partner_recv,
    left_back_send,
    left_back_recv,
    partner_back_send,
    partner_back_recv,
):
    blk, grp = lax.axis_index("blk"), lax.axis_index("grp")
    count = lax.axis_size("blk")
    right = (lax.rem(blk + 1, count), grp)
    left = (lax.rem(blk + count - 1, count), grp)
    partner = (blk, grp + 1 - 2 * lax.rem(grp, 2))

    first_core = lax.rem(blk, 2) == 0

    barrier = pltpu.get_barrier_semaphore()
    pl.semaphore_signal(barrier, inc=1, device_id=partner, device_id_type=MESH)

    @pl.when(jnp.logical_not(first_core))
    def _():
        pl.semaphore_signal(barrier, inc=1, device_id=right, device_id_type=MESH)
        pl.semaphore_signal(barrier, inc=1, device_id=left, device_id_type=MESH)

    @pl.when(first_core)
    def _():
        pl.semaphore_wait(barrier, 3)

    @pl.when(jnp.logical_not(first_core))
    def _():
        pl.semaphore_wait(barrier, 1)

    def remote(source, target, send, recv, device):
        return pltpu.make_async_remote_copy(source, target, send, recv, device_id=device, device_id_type=MESH)

    def text_copy(target, send, recv, device, i):
        rows = rows_of(i, STEP)
        return remote(caption_hbm.at[rows, :], target.at[rows, :], send.at[i], recv.at[i], device)

    to_partner = [text_copy(partner_text, partner_send, partner_recv, partner, i) for i in range(STEPS)]
    to_right = [text_copy(left_text, left_send, left_recv, right, i) for i in range(STEPS)]
    label_copies = [
        remote(labels_hbm, partner_labels, label_send.at[0], label_recv.at[0], partner),
        remote(labels_hbm, left_labels, label_send.at[1], label_recv.at[1], right),
    ]
    label_copies[0].start()
    for copy in to_partner:
        copy.start()

    loads = [
        pltpu.make_async_copy(source, target, local_sems.at[i])
        for i, (source, target) in enumerate(((labels_hbm, labels), (image_hbm, image), (caption_hbm, caption)))
    ]
    for load in loads:
        load.start()

    @pl.when(first_core)
    def _():
        pl.semaphore_signal(inside_sem, inc=1, device_id=left, device_id_type=MESH)

    def left_back(i):
        rows = rows_of(i, STEP)
        return remote(left_out.at[rows, :], left_in.at[rows, :], left_back_send.at[i], left_back_recv.at[i], left)

    def partner_back(i):
        rows = rows_of(i, PIECE)
        return remote(
            partner_out.at[rows, :], partner_in.at[rows, :], partner_back_send.at[i], partner_back_recv.at[i], partner
        )

    scale = jnp.exp(jnp.full((1, STEP), log_scale[0], jnp.float32))
    bias = offset[0]

    loads[0].wait()
    for i in range(ROWS // LANES):
        label_column[i * LANES : (i + 1) * LANES, :] = jnp.broadcast_to(labels[i : i + 1, :], (LANES, LANES)).T

    loads[1].wait()

    @pl.loop(0, PIECES)
    def _(i):
        rows = rows_of(i, PIECE)
        normalize_rows(image, rows, image_low, rows, image_inv)

    @pl.when(jnp.logical_not(first_core))
    def _():
        pl.semaphore_wait(inside_sem, 1)

    label_copies[1].start()
    for copy in to_right:
        copy.start()

    loads[2].wait()

    @pl.loop(0, PIECES)
    def _(i):
        rows = rows_of(i, PIECE)
        normalize_rows(caption, rows, text_low, rows, text_inv)

    def tile(step, text, text_rows, text_labels, first):
        per = STEP // LANES
        row = jnp.concatenate([text_labels[pl.ds(step * per + j, 1), :] for j in range(per)], axis=1)

        @pl.loop(0, ROWS // STEP)
        def _(m):
            rows = rows_of(m, STEP)
            images = image_low[rows, :]
            texts = text[text_rows, :]
            products = lax.dot_general(images, texts, (((1,), (1,)), ((), ())), preferred_element_type=jnp.float32)
            column = jnp.concatenate([label_column[rows, :]] * per, axis=1)
            positive = (column == row).astype(jnp.float32)
            weight = ((jax.nn.sigmoid(scale * products + bias) - positive) * scale).astype(jnp.bfloat16)
            update = jnp.dot(weight, texts, preferred_element_type=jnp.float32)

            @pl.when(jnp.logical_and(first, step == 0))
            def _():
                grad_image[rows, :] = update

            @pl.when(jnp.logical_not(jnp.logical_and(first, step == 0)))
            def _():
                grad_image[rows, :] += update

            back = lax.dot_general(weight, images, (((0,), (0,)), ((), ())), preferred_element_type=jnp.float32)

            @pl.when(m == 0)
            def _():
                part[...] = back

            @pl.when(m > 0)
            def _():
                part[...] += back

    @pl.loop(0, STEPS)
    def _(c):
        rows = rows_of(c, STEP)
        tile(c, text_low, rows, labels, True)
        grad_text[rows, :] = part[...]

    def normalize_arrived(text, c):
        @pl.loop(0, STEP // PIECE)
        def _(i):
            normalize_rows(text, rows_of(c * (STEP // PIECE) + i, PIECE), low, rows_of(i, PIECE))

    label_copies[1].wait()

    @pl.loop(0, STEPS)
    def _(c):
        text_copy(left_text, left_send, left_recv, right, c).wait_recv()
        normalize_arrived(left_text, c)
        tile(c, low, pl.ds(0, STEP), left_labels, False)
        left_out[rows_of(c, STEP), :] = part[...].astype(jnp.bfloat16)
        left_back(c).start()

    label_copies[0].wait()

    @pl.loop(0, STEPS)
    def _(c):
        text_copy(partner_text, partner_send, partner_recv, partner, c).wait_recv()
        normalize_arrived(partner_text, c)
        tile(c, low, pl.ds(0, STEP), partner_labels, False)
        partner_out[rows_of(c, STEP), :] = part[...].astype(jnp.bfloat16)
        for j in range(STEP // PIECE):
            partner_back(c * (STEP // PIECE) + j).start()

    def project_back(grad, source, inverse, rows, gradient):
        inv = inverse[rows, :]
        direction = source[rows, :].astype(jnp.float32) * inv
        along = jnp.sum(direction * gradient, axis=-1, keepdims=True)
        grad[rows, :] = inv * (gradient - direction * along)

    @pl.loop(0, PIECES)
    def _(i):
        rows = rows_of(i, PIECE)
        project_back(grad_image, image, image_inv, rows, grad_image[rows, :])

    @pl.loop(0, STEPS)
    def _(c):
        left_back(c).wait_recv()
        rows = rows_of(c, STEP)
        grad_text[rows, :] += left_in[rows, :].astype(jnp.float32)

    for c in range(STEPS):
        to_right[c].wait_send()
        to_partner[c].wait_send()
        left_back(c).wait_send()

    @pl.loop(0, PIECES)
    def _(i):
        partner_back(i).wait()
        rows = rows_of(i, PIECE)
        gradient = grad_text[rows, :] + partner_in[rows, :].astype(jnp.float32)
        project_back(grad_text, caption, text_inv, rows, gradient)


def write_out(grad_image, grad_text, image_out, text_out, sems):
    copies = [
        pltpu.make_async_copy(source.at[rows_of(i, ROWS // WRITES), :], target.at[rows_of(i, ROWS // WRITES), :], sems.at[j, i])
        for i in range(WRITES)
        for j, (source, target) in enumerate(((grad_image, image_out), (grad_text, text_out)))
    ]
    for copy in copies:
        copy.start()
    for copy in copies:
        copy.wait()


def local(image_vectors, caption_vectors, caption_labels, log_logit_scale, logit_offset_bias):
    block = (ROWS, WIDTH)
    label_block = (ROWS // LANES, LANES)
    hbm = pl.BlockSpec(memory_space=pltpu.HBM)
    smem = pl.BlockSpec(memory_space=pltpu.SMEM)
    vmem = pl.BlockSpec(memory_space=pltpu.VMEM)
    dma = pltpu.SemaphoreType.DMA
    low_block = pltpu.VMEM(block, jnp.bfloat16)
    grads = pl.pallas_call(
        kernel,
        out_shape=(pltpu.VMEM(block, jnp.float32), pltpu.VMEM(block, jnp.float32)),
        in_specs=[hbm, hbm, hbm, smem, smem],
        out_specs=(vmem, vmem),
        scratch_shapes=[
            low_block,
            low_block,
            pltpu.VMEM(label_block, jnp.int32),
            low_block,
            low_block,
            pltpu.VMEM((ROWS, 1), jnp.float32),
            pltpu.VMEM((ROWS, 1), jnp.float32),
            pltpu.VMEM((ROWS, LANES), jnp.int32),
            pltpu.VMEM(label_block, jnp.int32),
            pltpu.VMEM(label_block, jnp.int32),
            low_block,
            low_block,
            pltpu.VMEM((STEP, WIDTH), jnp.bfloat16),
            pltpu.VMEM((STEP, WIDTH), jnp.float32),
            low_block,
            low_block,
            low_block,
            low_block,
            dma((3,)),
            pltpu.SemaphoreType.REGULAR,
            dma((2,)),
            dma((2,)),
            dma((STEPS,)),
            dma((STEPS,)),
            dma((STEPS,)),
            dma((STEPS,)),
            dma((STEPS,)),
            dma((STEPS,)),
            dma((PIECES,)),
            dma((PIECES,)),
        ],
        compiler_params=pltpu.CompilerParams(
            collective_id=0, has_side_effects=True, vmem_limit_bytes=32 * 1024 * 1024
        ),
        cost_estimate=pl.CostEstimate(
            flops=18 * ROWS * ROWS * WIDTH, bytes_accessed=12 * ROWS * WIDTH, transcendentals=3 * ROWS * ROWS
        ),
        name="contrast",
    )(
        *(
            pltpu.with_memory_space_constraint(value, pltpu.HBM)
            for value in (
                image_vectors,
                caption_vectors,
                caption_labels.reshape(label_block),
            )
        ),
        log_logit_scale,
        logit_offset_bias,
    )
    return pl.pallas_call(
        write_out,
        out_shape=(jax.ShapeDtypeStruct(block, jnp.float32),) * 2,
        in_specs=[vmem] * 2,
        out_specs=(pl.BlockSpec(memory_space=pl.ANY),) * 2,
        scratch_shapes=[dma((2, WRITES))],
        compiler_params=pltpu.CompilerParams(vmem_limit_bytes=16 * 1024 * 1024),
        cost_estimate=pl.CostEstimate(flops=0, bytes_accessed=16 * ROWS * WIDTH, transcendentals=0),
        name="write_out",
    )(*(pltpu.with_memory_space_constraint(value, pltpu.VMEM) for value in grads))


def solution(mesh):
    rows = P(("blk", "grp"), None)
    return jax.shard_map(
        local, mesh=mesh, in_specs=(rows, rows, P(("blk", "grp")), P(), P()), out_specs=(rows, rows), check_vma=False
    )
```

```python
import jax
import jax.numpy as jnp
from jax import lax
from jax.experimental import pallas as pl
from jax.experimental.pallas import tpu as pltpu
from jax.sharding import PartitionSpec as P

ROWS = 768
WIDTH = 1152
STEP = 256
STEPS = ROWS // STEP
PIECE = 128
PIECES = ROWS // PIECE
LANES = 128
EARLY = 2
ENDS = tuple((i * PIECE, PIECE) for i in range(EARLY, PIECES - 1)) + ((640, 64), (704, 64))
MESH = pl.DeviceIdType.MESH


def rows_of(index, size):
    return pl.ds(pl.multiple_of(index * size, size), size)


def normalize_rows(source, rows, low, low_rows, inverse=None):
    values = source[rows, :].astype(jnp.float32)
    scaled = lax.rsqrt(jnp.sum(values * values, axis=-1, keepdims=True) + 1e-06)
    low[low_rows, :] = (values * scaled).astype(jnp.bfloat16)
    if inverse is not None:
        inverse[rows, :] = scaled


def kernel(
    image_hbm,
    caption_hbm,
    labels_hbm,
    log_scale,
    offset,
    grad_image,
    grad_text,
    partner_out,
    image,
    caption,
    labels,
    image_low,
    text_low,
    image_inv,
    text_inv,
    label_column,
    left_labels,
    partner_labels,
    left_text,
    partner_text,
    low,
    part,
    left_out,
    left_in,
    partner_in,
    local_sems,
    inside_sem,
    label_send,
    label_recv,
    left_send,
    left_recv,
    partner_send,
    partner_recv,
    left_back_send,
    left_back_recv,
    partner_back_send,
    partner_back_recv,
):
    blk, grp = lax.axis_index("blk"), lax.axis_index("grp")
    count = lax.axis_size("blk")
    right = (lax.rem(blk + 1, count), grp)
    left = (lax.rem(blk + count - 1, count), grp)
    partner = (blk, grp + 1 - 2 * lax.rem(grp, 2))

    first_core = lax.rem(blk, 2) == 0

    barrier = pltpu.get_barrier_semaphore()
    pl.semaphore_signal(barrier, inc=1, device_id=partner, device_id_type=MESH)

    @pl.when(jnp.logical_not(first_core))
    def _():
        pl.semaphore_signal(barrier, inc=1, device_id=right, device_id_type=MESH)
        pl.semaphore_signal(barrier, inc=1, device_id=left, device_id_type=MESH)

    @pl.when(first_core)
    def _():
        pl.semaphore_wait(barrier, 3)

    @pl.when(jnp.logical_not(first_core))
    def _():
        pl.semaphore_wait(barrier, 1)

    def remote(source, target, send, recv, device):
        return pltpu.make_async_remote_copy(source, target, send, recv, device_id=device, device_id_type=MESH)

    def text_copy(target, send, recv, device, i):
        rows = rows_of(i, STEP)
        return remote(caption_hbm.at[rows, :], target.at[rows, :], send.at[i], recv.at[i], device)

    to_partner = [text_copy(partner_text, partner_send, partner_recv, partner, i) for i in range(STEPS)]
    to_right = [text_copy(left_text, left_send, left_recv, right, i) for i in range(STEPS)]
    label_copies = [
        remote(labels_hbm, partner_labels, label_send.at[0], label_recv.at[0], partner),
        remote(labels_hbm, left_labels, label_send.at[1], label_recv.at[1], right),
    ]
    def send_right():
        label_copies[1].start()
        for copy in to_right:
            copy.start()

    @pl.when(first_core)
    def _():
        pl.semaphore_signal(inside_sem, inc=1, device_id=left, device_id_type=MESH)
        send_right()

    label_copies[0].start()
    for copy in to_partner:
        copy.start()

    loads = [
        pltpu.make_async_copy(source, target, local_sems.at[i])
        for i, (source, target) in enumerate(((labels_hbm, labels), (image_hbm, image), (caption_hbm, caption)))
    ]
    for load in loads:
        load.start()

    def left_back(i):
        rows = rows_of(i, STEP)
        return remote(left_out.at[rows, :], left_in.at[rows, :], left_back_send.at[i], left_back_recv.at[i], left)

    def partner_back(i):
        rows = rows_of(i, PIECE)
        return remote(
            partner_out.at[rows, :], partner_in.at[rows, :], partner_back_send.at[i], partner_back_recv.at[i], partner
        )

    scale = jnp.exp(jnp.full((1, STEP), log_scale[0], jnp.float32))
    bias = offset[0]

    loads[0].wait()
    for i in range(ROWS // LANES):
        label_column[i * LANES : (i + 1) * LANES, :] = jnp.broadcast_to(labels[i : i + 1, :], (LANES, LANES)).T

    loads[1].wait()

    @pl.loop(0, PIECES)
    def _(i):
        rows = rows_of(i, PIECE)
        normalize_rows(image, rows, image_low, rows, image_inv)

    @pl.when(jnp.logical_not(first_core))
    def _():
        pl.semaphore_wait(inside_sem, 1)
        send_right()

    loads[2].wait()

    @pl.loop(0, PIECES)
    def _(i):
        rows = rows_of(i, PIECE)
        normalize_rows(caption, rows, text_low, rows, text_inv)

    def tile(step, text, text_rows, text_labels, first):
        per = STEP // LANES
        row = jnp.concatenate([text_labels[pl.ds(step * per + j, 1), :] for j in range(per)], axis=1)

        @pl.loop(0, ROWS // STEP)
        def _(m):
            rows = rows_of(m, STEP)
            images = image_low[rows, :]
            texts = text[text_rows, :]
            products = lax.dot_general(images, texts, (((1,), (1,)), ((), ())), preferred_element_type=jnp.float32)
            column = jnp.concatenate([label_column[rows, :]] * per, axis=1)
            positive = (column == row).astype(jnp.float32)
            weight = ((jax.nn.sigmoid(scale * products + bias) - positive) * scale).astype(jnp.bfloat16)
            update = jnp.dot(weight, texts, preferred_element_type=jnp.float32)

            @pl.when(jnp.logical_and(first, step == 0))
            def _():
                grad_image[rows, :] = update

            @pl.when(jnp.logical_not(jnp.logical_and(first, step == 0)))
            def _():
                grad_image[rows, :] += update

            back = lax.dot_general(weight, images, (((0,), (0,)), ((), ())), preferred_element_type=jnp.float32)

            @pl.when(m == 0)
            def _():
                part[...] = back

            @pl.when(m > 0)
            def _():
                part[...] += back

    @pl.loop(0, STEPS)
    def _(c):
        rows = rows_of(c, STEP)
        tile(c, text_low, rows, labels, True)
        grad_text[rows, :] = part[...]

    def normalize_arrived(text, c):
        @pl.loop(0, STEP // PIECE)
        def _(i):
            normalize_rows(text, rows_of(c * (STEP // PIECE) + i, PIECE), low, rows_of(i, PIECE))

    label_copies[1].wait()

    @pl.loop(0, STEPS)
    def _(c):
        text_copy(left_text, left_send, left_recv, right, c).wait_recv()
        normalize_arrived(left_text, c)
        tile(c, low, pl.ds(0, STEP), left_labels, False)
        left_out[rows_of(c, STEP), :] = part[...].astype(jnp.bfloat16)
        left_back(c).start()

    label_copies[0].wait()

    @pl.loop(0, STEPS)
    def _(c):
        text_copy(partner_text, partner_send, partner_recv, partner, c).wait_recv()
        normalize_arrived(partner_text, c)
        tile(c, low, pl.ds(0, STEP), partner_labels, False)
        partner_out[rows_of(c, STEP), :] = part[...].astype(jnp.bfloat16)

        for j in range(STEP // PIECE):
            piece = c * (STEP // PIECE) + j

            @pl.when(jnp.logical_or(first_core, piece < EARLY))
            def _():
                partner_back(piece).start()

    @pl.loop(0, PIECES)
    def _(i):
        rows = rows_of(i, PIECE)
        grad_image[rows, :] = project_back(image[rows, :], image_inv[rows, :], grad_image[rows, :])

    @pl.loop(0, STEPS)
    def _(c):
        left_back(c).wait_recv()
        rows = rows_of(c, STEP)
        grad_text[rows, :] += left_in[rows, :].astype(jnp.float32)

    for c in range(STEPS):
        to_right[c].wait_send()
        to_partner[c].wait_send()
        left_back(c).wait_send()

    @pl.loop(0, jnp.where(first_core, PIECES, EARLY))
    def _(i):
        partner_back(i).wait()
        rows = rows_of(i, PIECE)
        gradient = grad_text[rows, :] + partner_in[rows, :].astype(jnp.float32)
        grad_text[rows, :] = project_back(caption[rows, :], text_inv[rows, :], gradient)


def project_back(source, inv, gradient):
    direction = source.astype(jnp.float32) * inv
    along = jnp.sum(direction * gradient, axis=-1, keepdims=True)
    return inv * (gradient - direction * along)


def finish(caption_hbm, grad_in, partner_out, image_out, grad_text, caption, partner_in, load_sem, send, recv):
    blk, grp = lax.axis_index("blk"), lax.axis_index("grp")
    partner = (blk, grp + 1 - 2 * lax.rem(grp, 2))
    first_core = lax.rem(blk, 2) == 0
    barrier = pltpu.get_barrier_semaphore()
    load = pltpu.make_async_copy(caption_hbm, caption, load_sem)

    @pl.when(jnp.logical_not(first_core))
    def _():
        pl.semaphore_signal(barrier, inc=1, device_id=partner, device_id_type=MESH)
        load.start()
        pl.semaphore_wait(barrier, 1)

    def back(i):
        rows = pl.ds(*ENDS[i])
        return pltpu.make_async_remote_copy(
            partner_out.at[rows, :],
            partner_in.at[rows, :],
            send.at[i],
            recv.at[i],
            device_id=partner,
            device_id_type=MESH,
        )

    def rows_back(rows, source):
        values = caption[rows, :].astype(jnp.float32)
        inv = lax.rsqrt(jnp.sum(values * values, axis=-1, keepdims=True) + 1e-06)
        gradient = grad_in[rows, :] + source[rows, :].astype(jnp.float32)
        grad_text[rows, :] = project_back(caption[rows, :], inv, gradient)

    def done_rows(pieces):
        @pl.loop(0, pieces)
        def _(i):
            rows = rows_of(i, PIECE)
            grad_text[rows, :] = grad_in[rows, :]

    @pl.when(jnp.logical_not(first_core))
    def _():
        copies = [back(i) for i in range(len(ENDS))]
        for copy in copies:
            copy.start()
        done_rows(EARLY)
        load.wait()
        for copy, end in zip(copies, ENDS):
            copy.wait_recv()
            rows_back(pl.ds(*end), partner_in)
        for copy in copies:
            copy.wait_send()

    @pl.when(first_core)
    def _():
        done_rows(PIECES)


def write_out(source, target, sem):
    copy = pltpu.make_async_copy(source, target, sem)
    copy.start()
    copy.wait()


def written(value):
    return pl.pallas_call(
        write_out,
        out_shape=jax.ShapeDtypeStruct(value.shape, value.dtype),
        in_specs=[pl.BlockSpec(memory_space=pltpu.VMEM)],
        out_specs=pl.BlockSpec(memory_space=pl.ANY),
        scratch_shapes=[pltpu.SemaphoreType.DMA(())],
        compiler_params=pltpu.CompilerParams(vmem_limit_bytes=4 * 1024 * 1024),
        cost_estimate=pl.CostEstimate(flops=0, bytes_accessed=8 * ROWS * WIDTH, transcendentals=0),
        name="write_out",
    )(pltpu.with_memory_space_constraint(value, pltpu.VMEM))


def local(image_vectors, caption_vectors, caption_labels, log_logit_scale, logit_offset_bias):
    block = (ROWS, WIDTH)
    label_block = (ROWS // LANES, LANES)
    hbm = pl.BlockSpec(memory_space=pltpu.HBM)
    smem = pl.BlockSpec(memory_space=pltpu.SMEM)
    vmem = pl.BlockSpec(memory_space=pltpu.VMEM)
    dma = pltpu.SemaphoreType.DMA
    low_block = pltpu.VMEM(block, jnp.bfloat16)
    captions = pltpu.with_memory_space_constraint(caption_vectors, pltpu.HBM)
    grad_image, grad_text, partner_out = pl.pallas_call(
        kernel,
        out_shape=(pltpu.VMEM(block, jnp.float32),) * 2 + (low_block,),
        in_specs=[hbm, hbm, hbm, smem, smem],
        out_specs=(vmem,) * 3,
        scratch_shapes=[
            low_block,
            low_block,
            pltpu.VMEM(label_block, jnp.int32),
            low_block,
            low_block,
            pltpu.VMEM((ROWS, 1), jnp.float32),
            pltpu.VMEM((ROWS, 1), jnp.float32),
            pltpu.VMEM((ROWS, LANES), jnp.int32),
            pltpu.VMEM(label_block, jnp.int32),
            pltpu.VMEM(label_block, jnp.int32),
            low_block,
            low_block,
            pltpu.VMEM((STEP, WIDTH), jnp.bfloat16),
            pltpu.VMEM((STEP, WIDTH), jnp.float32),
            low_block,
            low_block,
            low_block,
            dma((3,)),
            pltpu.SemaphoreType.REGULAR,
            dma((2,)),
            dma((2,)),
            dma((STEPS,)),
            dma((STEPS,)),
            dma((STEPS,)),
            dma((STEPS,)),
            dma((STEPS,)),
            dma((STEPS,)),
            dma((PIECES,)),
            dma((PIECES,)),
        ],
        compiler_params=pltpu.CompilerParams(
            collective_id=0, has_side_effects=True, vmem_limit_bytes=32 * 1024 * 1024
        ),
        cost_estimate=pl.CostEstimate(
            flops=18 * ROWS * ROWS * WIDTH, bytes_accessed=12 * ROWS * WIDTH, transcendentals=3 * ROWS * ROWS
        ),
        name="contrast",
    )(
        *(
            pltpu.with_memory_space_constraint(value, pltpu.HBM)
            for value in (
                image_vectors,
                caption_vectors,
                caption_labels.reshape(label_block),
            )
        ),
        log_logit_scale,
        logit_offset_bias,
    )
    image_out = written(grad_image)
    grad_text = pl.pallas_call(
        finish,
        out_shape=pltpu.VMEM(block, jnp.float32),
        in_specs=[hbm, vmem, vmem, hbm],
        out_specs=vmem,
        scratch_shapes=[low_block, low_block, dma(()), dma((len(ENDS),)), dma((len(ENDS),))],
        compiler_params=pltpu.CompilerParams(
            collective_id=1, has_side_effects=True, vmem_limit_bytes=16 * 1024 * 1024
        ),
        cost_estimate=pl.CostEstimate(flops=ROWS * WIDTH, bytes_accessed=8 * ROWS * WIDTH, transcendentals=0),
        name="finish",
    )(captions, *(pltpu.with_memory_space_constraint(v, pltpu.VMEM) for v in (grad_text, partner_out)), pltpu.with_memory_space_constraint(image_out, pltpu.HBM))
    return image_out, written(grad_text)


def solution(mesh):
    rows = P(("blk", "grp"), None)
    return jax.shard_map(
        local, mesh=mesh, in_specs=(rows, rows, P(("blk", "grp")), P(), P()), out_specs=(rows, rows), check_vma=False
    )
```

```python
import jax
import jax.numpy as jnp
from jax import lax
from jax.experimental import pallas as pl
from jax.experimental.pallas import tpu as pltpu
from jax.sharding import PartitionSpec as P

ROWS = 768
WIDTH = 1152
STEP = 256
STEPS = ROWS // STEP
PIECE = 128
PIECES = ROWS // PIECE
LANES = 128
EARLY = 2
ENDS = tuple((i * PIECE, PIECE) for i in range(EARLY, PIECES - 1)) + ((640, 64), (704, 64))
MESH = pl.DeviceIdType.MESH


def rows_of(index, size):
    return pl.ds(pl.multiple_of(index * size, size), size)


def normalize_rows(source, rows, low, low_rows, inverse=None):
    values = source[rows, :].astype(jnp.float32)
    scaled = lax.rsqrt(jnp.sum(values * values, axis=-1, keepdims=True) + 1e-06)
    low[low_rows, :] = (values * scaled).astype(jnp.bfloat16)
    if inverse is not None:
        inverse[rows, :] = scaled


def kernel(
    image_hbm,
    caption_hbm,
    labels_hbm,
    log_scale,
    offset,
    grad_image,
    grad_text,
    partner_out,
    image,
    caption,
    labels,
    image_low,
    text_low,
    image_inv,
    text_inv,
    label_column,
    left_labels,
    partner_labels,
    left_text,
    partner_text,
    low,
    part,
    left_out,
    left_in,
    partner_in,
    local_sems,
    inside_sem,
    label_send,
    label_recv,
    left_send,
    left_recv,
    partner_send,
    partner_recv,
    left_back_send,
    left_back_recv,
    partner_back_send,
    partner_back_recv,
):
    blk, grp = lax.axis_index("blk"), lax.axis_index("grp")
    count = lax.axis_size("blk")
    right = (lax.rem(blk + 1, count), grp)
    left = (lax.rem(blk + count - 1, count), grp)
    partner = (blk, grp + 1 - 2 * lax.rem(grp, 2))

    first_core = lax.rem(blk, 2) == 0

    barrier = pltpu.get_barrier_semaphore()
    pl.semaphore_signal(barrier, inc=1, device_id=partner, device_id_type=MESH)

    @pl.when(jnp.logical_not(first_core))
    def _():
        pl.semaphore_signal(barrier, inc=1, device_id=right, device_id_type=MESH)
        pl.semaphore_signal(barrier, inc=1, device_id=left, device_id_type=MESH)

    @pl.when(first_core)
    def _():
        pl.semaphore_wait(barrier, 3)

    @pl.when(jnp.logical_not(first_core))
    def _():
        pl.semaphore_wait(barrier, 1)

    def remote(source, target, send, recv, device):
        return pltpu.make_async_remote_copy(source, target, send, recv, device_id=device, device_id_type=MESH)

    def text_copy(target, send, recv, device, i):
        rows = rows_of(i, STEP)
        return remote(caption_hbm.at[rows, :], target.at[rows, :], send.at[i], recv.at[i], device)

    to_partner = [text_copy(partner_text, partner_send, partner_recv, partner, i) for i in range(STEPS)]
    to_right = [text_copy(left_text, left_send, left_recv, right, i) for i in range(STEPS)]
    label_copies = [
        remote(labels_hbm, partner_labels, label_send.at[0], label_recv.at[0], partner),
        remote(labels_hbm, left_labels, label_send.at[1], label_recv.at[1], right),
    ]
    def send_right():
        label_copies[1].start()
        for copy in to_right:
            copy.start()

    @pl.when(first_core)
    def _():
        pl.semaphore_signal(inside_sem, inc=1, device_id=left, device_id_type=MESH)
        send_right()

    label_copies[0].start()
    for copy in to_partner:
        copy.start()

    loads = [
        pltpu.make_async_copy(source, target, local_sems.at[i])
        for i, (source, target) in enumerate(((labels_hbm, labels), (image_hbm, image), (caption_hbm, caption)))
    ]
    for load in loads:
        load.start()

    def left_back(i):
        rows = rows_of(i, STEP)
        return remote(left_out.at[rows, :], left_in.at[rows, :], left_back_send.at[i], left_back_recv.at[i], left)

    def partner_back(i):
        rows = rows_of(i, PIECE)
        return remote(
            partner_out.at[rows, :], partner_in.at[rows, :], partner_back_send.at[i], partner_back_recv.at[i], partner
        )

    scale = jnp.exp(jnp.full((1, STEP), log_scale[0], jnp.float32))
    bias = offset[0]

    loads[0].wait()
    for i in range(ROWS // LANES):
        label_column[i * LANES : (i + 1) * LANES, :] = jnp.broadcast_to(labels[i : i + 1, :], (LANES, LANES)).T

    loads[1].wait()

    @pl.loop(0, PIECES)
    def _(i):
        rows = rows_of(i, PIECE)
        normalize_rows(image, rows, image_low, rows, image_inv)

    @pl.when(jnp.logical_not(first_core))
    def _():
        pl.semaphore_wait(inside_sem, 1)
        send_right()

    loads[2].wait()

    @pl.loop(0, PIECES)
    def _(i):
        rows = rows_of(i, PIECE)
        normalize_rows(caption, rows, text_low, rows, text_inv)

    def tile(step, text, text_rows, text_labels, first):
        per = STEP // LANES
        row = jnp.concatenate([text_labels[pl.ds(step * per + j, 1), :] for j in range(per)], axis=1)

        @pl.loop(0, ROWS // STEP)
        def _(m):
            rows = rows_of(m, STEP)
            images = image_low[rows, :]
            texts = text[text_rows, :]
            products = lax.dot_general(images, texts, (((1,), (1,)), ((), ())), preferred_element_type=jnp.float32)
            column = jnp.concatenate([label_column[rows, :]] * per, axis=1)
            positive = (column == row).astype(jnp.float32)
            weight = ((jax.nn.sigmoid(scale * products + bias) - positive) * scale).astype(jnp.bfloat16)
            update = jnp.dot(weight, texts, preferred_element_type=jnp.float32)

            @pl.when(jnp.logical_and(first, step == 0))
            def _():
                grad_image[rows, :] = update

            @pl.when(jnp.logical_not(jnp.logical_and(first, step == 0)))
            def _():
                grad_image[rows, :] += update

            back = lax.dot_general(weight, images, (((0,), (0,)), ((), ())), preferred_element_type=jnp.float32)

            @pl.when(m == 0)
            def _():
                part[...] = back

            @pl.when(m > 0)
            def _():
                part[...] += back

    @pl.loop(0, STEPS)
    def _(c):
        rows = rows_of(c, STEP)
        tile(c, text_low, rows, labels, True)
        grad_text[rows, :] = part[...]

    def normalize_arrived(text, c):
        @pl.loop(0, STEP // PIECE)
        def _(i):
            normalize_rows(text, rows_of(c * (STEP // PIECE) + i, PIECE), low, rows_of(i, PIECE))

    label_copies[1].wait()

    @pl.loop(0, STEPS)
    def _(c):
        text_copy(left_text, left_send, left_recv, right, c).wait_recv()
        normalize_arrived(left_text, c)
        tile(c, low, pl.ds(0, STEP), left_labels, False)
        left_out[rows_of(c, STEP), :] = part[...].astype(jnp.bfloat16)
        left_back(c).start()

    label_copies[0].wait()

    @pl.loop(0, STEPS)
    def _(c):
        text_copy(partner_text, partner_send, partner_recv, partner, c).wait_recv()
        normalize_arrived(partner_text, c)
        tile(c, low, pl.ds(0, STEP), partner_labels, False)
        partner_out[rows_of(c, STEP), :] = part[...].astype(jnp.bfloat16)

        for j in range(STEP // PIECE):
            piece = c * (STEP // PIECE) + j

            @pl.when(jnp.logical_or(first_core, piece < EARLY))
            def _():
                partner_back(piece).start()

    @pl.loop(0, PIECES)
    def _(i):
        rows = rows_of(i, PIECE)
        grad_image[rows, :] = project_back(image[rows, :], image_inv[rows, :], grad_image[rows, :])

    @pl.loop(0, STEPS)
    def _(c):
        left_back(c).wait_recv()
        rows = rows_of(c, STEP)
        grad_text[rows, :] += left_in[rows, :].astype(jnp.float32)

    for c in range(STEPS):
        to_right[c].wait_send()
        to_partner[c].wait_send()
        left_back(c).wait_send()

    @pl.loop(0, jnp.where(first_core, PIECES, EARLY))
    def _(i):
        partner_back(i).wait()
        rows = rows_of(i, PIECE)
        gradient = grad_text[rows, :] + partner_in[rows, :].astype(jnp.float32)
        grad_text[rows, :] = project_back(caption[rows, :], text_inv[rows, :], gradient)


def project_back(source, inv, gradient):
    direction = source.astype(jnp.float32) * inv
    along = jnp.sum(direction * gradient, axis=-1, keepdims=True)
    return inv * (gradient - direction * along)


def finish(caption_hbm, grad_in, partner_out, image_out, grad_text, caption, partner_in, load_sem, send, recv):
    blk, grp = lax.axis_index("blk"), lax.axis_index("grp")
    partner = (blk, grp + 1 - 2 * lax.rem(grp, 2))
    first_core = lax.rem(blk, 2) == 0
    barrier = pltpu.get_barrier_semaphore()
    load = pltpu.make_async_copy(caption_hbm, caption, load_sem)

    @pl.when(jnp.logical_not(first_core))
    def _():
        pl.semaphore_signal(barrier, inc=1, device_id=partner, device_id_type=MESH)
        load.start()
        pl.semaphore_wait(barrier, 1)

    def back(i):
        rows = pl.ds(*ENDS[i])
        return pltpu.make_async_remote_copy(
            partner_out.at[rows, :],
            partner_in.at[rows, :],
            send.at[i],
            recv.at[i],
            device_id=partner,
            device_id_type=MESH,
        )

    def rows_back(start, size, source):
        rows = pl.ds(start, size)
        values = caption[rows, :].astype(jnp.float32)
        inv = lax.rsqrt(jnp.sum(values * values, axis=-1, keepdims=True) + 1e-06)
        gradient = grad_in[rows, :] + source[rows, :].astype(jnp.float32)
        grad_text[pl.ds(start - EARLY * PIECE, size), :] = project_back(caption[rows, :], inv, gradient)

    def done_rows():
        @pl.loop(EARLY, PIECES)
        def _(i):
            rows = rows_of(i, PIECE)
            grad_text[rows_of(i - EARLY, PIECE), :] = grad_in[rows, :]

    @pl.when(jnp.logical_not(first_core))
    def _():
        copies = [back(i) for i in range(len(ENDS))]
        for copy in copies:
            copy.start()
        load.wait()
        for copy, end in zip(copies, ENDS):
            copy.wait_recv()
            rows_back(*end, partner_in)
        for copy in copies:
            copy.wait_send()

    @pl.when(first_core)
    def _():
        done_rows()


def write_early(grad_image, grad_text, image_out, text_out, sems):
    rows = pl.ds(0, EARLY * PIECE)
    copies = [
        pltpu.make_async_copy(grad_image, image_out, sems.at[0]),
        pltpu.make_async_copy(grad_text.at[rows, :], text_out.at[rows, :], sems.at[1]),
    ]
    for copy in copies:
        copy.start()
    for copy in copies:
        copy.wait()


def write_late(late, text_in, text_out, sem):
    copy = pltpu.make_async_copy(late, text_out.at[pl.ds(EARLY * PIECE, ROWS - EARLY * PIECE), :], sem)
    copy.start()
    copy.wait()


def local(image_vectors, caption_vectors, caption_labels, log_logit_scale, logit_offset_bias):
    block = (ROWS, WIDTH)
    label_block = (ROWS // LANES, LANES)
    hbm = pl.BlockSpec(memory_space=pltpu.HBM)
    smem = pl.BlockSpec(memory_space=pltpu.SMEM)
    vmem = pl.BlockSpec(memory_space=pltpu.VMEM)
    dma = pltpu.SemaphoreType.DMA
    low_block = pltpu.VMEM(block, jnp.bfloat16)
    captions = pltpu.with_memory_space_constraint(caption_vectors, pltpu.HBM)
    grad_image, grad_text, partner_out = pl.pallas_call(
        kernel,
        out_shape=(pltpu.VMEM(block, jnp.float32),) * 2 + (low_block,),
        in_specs=[hbm, hbm, hbm, smem, smem],
        out_specs=(vmem,) * 3,
        scratch_shapes=[
            low_block,
            low_block,
            pltpu.VMEM(label_block, jnp.int32),
            low_block,
            low_block,
            pltpu.VMEM((ROWS, 1), jnp.float32),
            pltpu.VMEM((ROWS, 1), jnp.float32),
            pltpu.VMEM((ROWS, LANES), jnp.int32),
            pltpu.VMEM(label_block, jnp.int32),
            pltpu.VMEM(label_block, jnp.int32),
            low_block,
            low_block,
            pltpu.VMEM((STEP, WIDTH), jnp.bfloat16),
            pltpu.VMEM((STEP, WIDTH), jnp.float32),
            low_block,
            low_block,
            low_block,
            dma((3,)),
            pltpu.SemaphoreType.REGULAR,
            dma((2,)),
            dma((2,)),
            dma((STEPS,)),
            dma((STEPS,)),
            dma((STEPS,)),
            dma((STEPS,)),
            dma((STEPS,)),
            dma((STEPS,)),
            dma((PIECES,)),
            dma((PIECES,)),
        ],
        compiler_params=pltpu.CompilerParams(
            collective_id=0, has_side_effects=True, vmem_limit_bytes=32 * 1024 * 1024
        ),
        cost_estimate=pl.CostEstimate(
            flops=18 * ROWS * ROWS * WIDTH, bytes_accessed=12 * ROWS * WIDTH, transcendentals=3 * ROWS * ROWS
        ),
        name="contrast",
    )(
        *(
            pltpu.with_memory_space_constraint(value, pltpu.HBM)
            for value in (
                image_vectors,
                caption_vectors,
                caption_labels.reshape(label_block),
            )
        ),
        log_logit_scale,
        logit_offset_bias,
    )
    any_space = pl.BlockSpec(memory_space=pl.ANY)
    whole = jax.ShapeDtypeStruct(block, jnp.float32)
    image_out, text_out = pl.pallas_call(
        write_early,
        out_shape=(whole, whole),
        in_specs=[vmem, vmem],
        out_specs=(any_space, any_space),
        scratch_shapes=[dma((2,))],
        compiler_params=pltpu.CompilerParams(vmem_limit_bytes=4 * 1024 * 1024),
        cost_estimate=pl.CostEstimate(flops=0, bytes_accessed=8 * ROWS * WIDTH, transcendentals=0),
        name="write_early",
    )(*(pltpu.with_memory_space_constraint(v, pltpu.VMEM) for v in (grad_image, grad_text)))
    late = pl.pallas_call(
        finish,
        out_shape=pltpu.VMEM((ROWS - EARLY * PIECE, WIDTH), jnp.float32),
        in_specs=[hbm, vmem, vmem, hbm],
        out_specs=vmem,
        scratch_shapes=[low_block, low_block, dma(()), dma((len(ENDS),)), dma((len(ENDS),))],
        compiler_params=pltpu.CompilerParams(
            collective_id=1, has_side_effects=True, vmem_limit_bytes=16 * 1024 * 1024
        ),
        cost_estimate=pl.CostEstimate(flops=ROWS * WIDTH, bytes_accessed=8 * ROWS * WIDTH, transcendentals=0),
        name="finish",
    )(
        captions,
        *(pltpu.with_memory_space_constraint(v, pltpu.VMEM) for v in (grad_text, partner_out)),
        pltpu.with_memory_space_constraint(image_out, pltpu.HBM),
    )
    text_out = pl.pallas_call(
        write_late,
        out_shape=whole,
        in_specs=[vmem, any_space],
        out_specs=any_space,
        scratch_shapes=[dma(())],
        input_output_aliases={1: 0},
        compiler_params=pltpu.CompilerParams(vmem_limit_bytes=4 * 1024 * 1024),
        cost_estimate=pl.CostEstimate(flops=0, bytes_accessed=8 * ROWS * WIDTH, transcendentals=0),
        name="write_late",
    )(pltpu.with_memory_space_constraint(late, pltpu.VMEM), text_out)
    return image_out, text_out


def solution(mesh):
    rows = P(("blk", "grp"), None)
    return jax.shard_map(
        local, mesh=mesh, in_specs=(rows, rows, P(("blk", "grp")), P(), P()), out_specs=(rows, rows), check_vma=False
    )
```

```python
import jax
import jax.numpy as jnp
from jax import lax
from jax.experimental import pallas as pl
from jax.experimental.pallas import tpu as pltpu
from jax.sharding import PartitionSpec as P

ROWS = 768
WIDTH = 1152
STEP = 256
STEPS = ROWS // STEP
PIECE = 128
PIECES = ROWS // PIECE
LANES = 128
EARLY = 2
ENDS = tuple((i * PIECE, PIECE) for i in range(EARLY, PIECES - 1)) + ((640, 64), (704, 64))
MESH = pl.DeviceIdType.MESH


def rows_of(index, size):
    return pl.ds(pl.multiple_of(index * size, size), size)


def normalize_rows(source, rows, low, low_rows, inverse=None):
    values = source[rows, :].astype(jnp.float32)
    scaled = lax.rsqrt(jnp.sum(values * values, axis=-1, keepdims=True) + 1e-06)
    low[low_rows, :] = (values * scaled).astype(jnp.bfloat16)
    if inverse is not None:
        inverse[rows, :] = scaled


def kernel(
    image_hbm,
    caption_hbm,
    labels_hbm,
    log_scale,
    offset,
    grad_image,
    grad_text,
    partner_out,
    image,
    caption,
    labels,
    image_low,
    text_low,
    image_inv,
    text_inv,
    label_column,
    left_labels,
    partner_labels,
    left_text,
    partner_text,
    low,
    part,
    left_out,
    left_in,
    partner_in,
    local_sems,
    inside_sem,
    label_send,
    label_recv,
    left_send,
    left_recv,
    partner_send,
    partner_recv,
    left_back_send,
    left_back_recv,
    partner_back_send,
    partner_back_recv,
):
    blk, grp = lax.axis_index("blk"), lax.axis_index("grp")
    count = lax.axis_size("blk")
    right = (lax.rem(blk + 1, count), grp)
    left = (lax.rem(blk + count - 1, count), grp)
    partner = (blk, grp + 1 - 2 * lax.rem(grp, 2))

    first_core = lax.rem(blk, 2) == 0

    barrier = pltpu.get_barrier_semaphore()
    pl.semaphore_signal(barrier, inc=1, device_id=partner, device_id_type=MESH)

    @pl.when(jnp.logical_not(first_core))
    def _():
        pl.semaphore_signal(barrier, inc=1, device_id=right, device_id_type=MESH)
        pl.semaphore_signal(barrier, inc=1, device_id=left, device_id_type=MESH)

    @pl.when(first_core)
    def _():
        pl.semaphore_wait(barrier, 3)

    @pl.when(jnp.logical_not(first_core))
    def _():
        pl.semaphore_wait(barrier, 1)

    def remote(source, target, send, recv, device):
        return pltpu.make_async_remote_copy(source, target, send, recv, device_id=device, device_id_type=MESH)

    def text_copy(target, send, recv, device, i):
        rows = rows_of(i, STEP)
        return remote(caption_hbm.at[rows, :], target.at[rows, :], send.at[i], recv.at[i], device)

    to_partner = [text_copy(partner_text, partner_send, partner_recv, partner, i) for i in range(STEPS)]
    to_right = [text_copy(left_text, left_send, left_recv, right, i) for i in range(STEPS)]
    label_copies = [
        remote(labels_hbm, partner_labels, label_send.at[0], label_recv.at[0], partner),
        remote(labels_hbm, left_labels, label_send.at[1], label_recv.at[1], right),
    ]
    def send_right():
        label_copies[1].start()
        for copy in to_right:
            copy.start()

    @pl.when(first_core)
    def _():
        pl.semaphore_signal(inside_sem, inc=1, device_id=left, device_id_type=MESH)
        send_right()

    label_copies[0].start()
    for copy in to_partner:
        copy.start()

    loads = [
        pltpu.make_async_copy(source, target, local_sems.at[i])
        for i, (source, target) in enumerate(((labels_hbm, labels), (image_hbm, image), (caption_hbm, caption)))
    ]
    for load in loads:
        load.start()

    def left_back(i):
        rows = rows_of(i, STEP)
        return remote(left_out.at[rows, :], left_in.at[rows, :], left_back_send.at[i], left_back_recv.at[i], left)

    def partner_back(i):
        rows = rows_of(i, PIECE)
        return remote(
            partner_out.at[rows, :], partner_in.at[rows, :], partner_back_send.at[i], partner_back_recv.at[i], partner
        )

    scale = jnp.exp(jnp.full((1, STEP), log_scale[0], jnp.float32))
    bias = offset[0]

    loads[0].wait()
    for i in range(ROWS // LANES):
        label_column[i * LANES : (i + 1) * LANES, :] = jnp.broadcast_to(labels[i : i + 1, :], (LANES, LANES)).T

    loads[1].wait()

    @pl.loop(0, PIECES)
    def _(i):
        rows = rows_of(i, PIECE)
        normalize_rows(image, rows, image_low, rows, image_inv)

    @pl.when(jnp.logical_not(first_core))
    def _():
        pl.semaphore_wait(inside_sem, 1)
        send_right()

    loads[2].wait()

    @pl.loop(0, PIECES)
    def _(i):
        rows = rows_of(i, PIECE)
        normalize_rows(caption, rows, text_low, rows, text_inv)

    def tile(step, text, text_rows, text_labels, first):
        per = STEP // LANES
        row = jnp.concatenate([text_labels[pl.ds(step * per + j, 1), :] for j in range(per)], axis=1)

        @pl.loop(0, ROWS // STEP)
        def _(m):
            rows = rows_of(m, STEP)
            images = image_low[rows, :]
            texts = text[text_rows, :]
            products = lax.dot_general(images, texts, (((1,), (1,)), ((), ())), preferred_element_type=jnp.float32)
            column = jnp.concatenate([label_column[rows, :]] * per, axis=1)
            positive = (column == row).astype(jnp.float32)
            weight = ((jax.nn.sigmoid(scale * products + bias) - positive) * scale).astype(jnp.bfloat16)
            update = jnp.dot(weight, texts, preferred_element_type=jnp.float32)

            @pl.when(jnp.logical_and(first, step == 0))
            def _():
                grad_image[rows, :] = update

            @pl.when(jnp.logical_not(jnp.logical_and(first, step == 0)))
            def _():
                grad_image[rows, :] += update

            back = lax.dot_general(weight, images, (((0,), (0,)), ((), ())), preferred_element_type=jnp.float32)

            @pl.when(m == 0)
            def _():
                part[...] = back

            @pl.when(m > 0)
            def _():
                part[...] += back

    @pl.loop(0, STEPS)
    def _(c):
        rows = rows_of(c, STEP)
        tile(c, text_low, rows, labels, True)
        grad_text[rows, :] = part[...]

    def normalize_arrived(text, c):
        @pl.loop(0, STEP // PIECE)
        def _(i):
            normalize_rows(text, rows_of(c * (STEP // PIECE) + i, PIECE), low, rows_of(i, PIECE))

    label_copies[1].wait()

    @pl.loop(0, STEPS)
    def _(c):
        text_copy(left_text, left_send, left_recv, right, c).wait_recv()
        normalize_arrived(left_text, c)
        tile(c, low, pl.ds(0, STEP), left_labels, False)
        left_out[rows_of(c, STEP), :] = part[...].astype(jnp.bfloat16)
        left_back(c).start()

    label_copies[0].wait()

    @pl.loop(0, STEPS)
    def _(c):
        text_copy(partner_text, partner_send, partner_recv, partner, c).wait_recv()
        normalize_arrived(partner_text, c)
        tile(c, low, pl.ds(0, STEP), partner_labels, False)
        partner_out[rows_of(c, STEP), :] = part[...].astype(jnp.bfloat16)

        for j in range(STEP // PIECE):
            piece = c * (STEP // PIECE) + j

            @pl.when(jnp.logical_or(first_core, piece < EARLY))
            def _():
                partner_back(piece).start()

    @pl.loop(0, PIECES)
    def _(i):
        rows = rows_of(i, PIECE)
        grad_image[rows, :] = project_back(image[rows, :], image_inv[rows, :], grad_image[rows, :])

    @pl.loop(0, STEPS)
    def _(c):
        left_back(c).wait_recv()
        rows = rows_of(c, STEP)
        grad_text[rows, :] += left_in[rows, :].astype(jnp.float32)

    for c in range(STEPS):
        to_right[c].wait_send()
        to_partner[c].wait_send()
        left_back(c).wait_send()

    @pl.loop(0, jnp.where(first_core, PIECES, EARLY))
    def _(i):
        partner_back(i).wait()
        rows = rows_of(i, PIECE)
        gradient = grad_text[rows, :] + partner_in[rows, :].astype(jnp.float32)
        grad_text[rows, :] = project_back(caption[rows, :], text_inv[rows, :], gradient)


def project_back(source, inv, gradient):
    direction = source.astype(jnp.float32) * inv
    along = jnp.sum(direction * gradient, axis=-1, keepdims=True)
    return inv * (gradient - direction * along)


def finish(caption_hbm, grad_in, partner_out, image_out, grad_text, caption, partner_in, load_sem, send, recv):
    blk, grp = lax.axis_index("blk"), lax.axis_index("grp")
    partner = (blk, grp + 1 - 2 * lax.rem(grp, 2))
    first_core = lax.rem(blk, 2) == 0
    barrier = pltpu.get_barrier_semaphore()
    load = pltpu.make_async_copy(caption_hbm, caption, load_sem)

    @pl.when(jnp.logical_not(first_core))
    def _():
        pl.semaphore_signal(barrier, inc=1, device_id=partner, device_id_type=MESH)
        load.start()
        pl.semaphore_wait(barrier, 1)

    def back(i):
        rows = pl.ds(*ENDS[i])
        return pltpu.make_async_remote_copy(
            partner_out.at[rows, :],
            partner_in.at[rows, :],
            send.at[i],
            recv.at[i],
            device_id=partner,
            device_id_type=MESH,
        )

    def rows_back(start, size, source):
        rows = pl.ds(start, size)
        values = caption[rows, :].astype(jnp.float32)
        inv = lax.rsqrt(jnp.sum(values * values, axis=-1, keepdims=True) + 1e-06)
        gradient = grad_in[rows, :] + source[rows, :].astype(jnp.float32)
        grad_text[pl.ds(start - EARLY * PIECE, size), :] = project_back(caption[rows, :], inv, gradient)

    @pl.when(jnp.logical_not(first_core))
    def _():
        copies = [back(i) for i in range(len(ENDS))]
        for copy in copies:
            copy.start()
        load.wait()
        for copy, end in zip(copies, ENDS):
            copy.wait_recv()
            rows_back(*end, partner_in)
        for copy in copies:
            copy.wait_send()


def write_early(grad_image, grad_text, image_out, text_out, sems):
    early, late = pl.ds(0, EARLY * PIECE), pl.ds(EARLY * PIECE, ROWS - EARLY * PIECE)
    copies = [
        pltpu.make_async_copy(grad_image, image_out, sems.at[0]),
        pltpu.make_async_copy(grad_text.at[early, :], text_out.at[early, :], sems.at[1]),
    ]
    for copy in copies:
        copy.start()

    @pl.when(lax.rem(lax.axis_index("blk"), 2) == 0)
    def _():
        rest = pltpu.make_async_copy(grad_text.at[late, :], text_out.at[late, :], sems.at[2])
        rest.start()
        rest.wait()

    for copy in copies:
        copy.wait()


def write_late(late, text_in, text_out, sem):
    @pl.when(lax.rem(lax.axis_index("blk"), 2) == 1)
    def _():
        copy = pltpu.make_async_copy(late, text_out.at[pl.ds(EARLY * PIECE, ROWS - EARLY * PIECE), :], sem)
        copy.start()
        copy.wait()


def local(image_vectors, caption_vectors, caption_labels, log_logit_scale, logit_offset_bias):
    block = (ROWS, WIDTH)
    label_block = (ROWS // LANES, LANES)
    hbm = pl.BlockSpec(memory_space=pltpu.HBM)
    smem = pl.BlockSpec(memory_space=pltpu.SMEM)
    vmem = pl.BlockSpec(memory_space=pltpu.VMEM)
    dma = pltpu.SemaphoreType.DMA
    low_block = pltpu.VMEM(block, jnp.bfloat16)
    captions = pltpu.with_memory_space_constraint(caption_vectors, pltpu.HBM)
    grad_image, grad_text, partner_out = pl.pallas_call(
        kernel,
        out_shape=(pltpu.VMEM(block, jnp.float32),) * 2 + (low_block,),
        in_specs=[hbm, hbm, hbm, smem, smem],
        out_specs=(vmem,) * 3,
        scratch_shapes=[
            low_block,
            low_block,
            pltpu.VMEM(label_block, jnp.int32),
            low_block,
            low_block,
            pltpu.VMEM((ROWS, 1), jnp.float32),
            pltpu.VMEM((ROWS, 1), jnp.float32),
            pltpu.VMEM((ROWS, LANES), jnp.int32),
            pltpu.VMEM(label_block, jnp.int32),
            pltpu.VMEM(label_block, jnp.int32),
            low_block,
            low_block,
            pltpu.VMEM((STEP, WIDTH), jnp.bfloat16),
            pltpu.VMEM((STEP, WIDTH), jnp.float32),
            low_block,
            low_block,
            low_block,
            dma((3,)),
            pltpu.SemaphoreType.REGULAR,
            dma((2,)),
            dma((2,)),
            dma((STEPS,)),
            dma((STEPS,)),
            dma((STEPS,)),
            dma((STEPS,)),
            dma((STEPS,)),
            dma((STEPS,)),
            dma((PIECES,)),
            dma((PIECES,)),
        ],
        compiler_params=pltpu.CompilerParams(
            collective_id=0, has_side_effects=True, vmem_limit_bytes=32 * 1024 * 1024
        ),
        cost_estimate=pl.CostEstimate(
            flops=18 * ROWS * ROWS * WIDTH, bytes_accessed=12 * ROWS * WIDTH, transcendentals=3 * ROWS * ROWS
        ),
        name="contrast",
    )(
        *(
            pltpu.with_memory_space_constraint(value, pltpu.HBM)
            for value in (
                image_vectors,
                caption_vectors,
                caption_labels.reshape(label_block),
            )
        ),
        log_logit_scale,
        logit_offset_bias,
    )
    any_space = pl.BlockSpec(memory_space=pl.ANY)
    whole = jax.ShapeDtypeStruct(block, jnp.float32)
    image_out, text_out = pl.pallas_call(
        write_early,
        out_shape=(whole, whole),
        in_specs=[vmem, vmem],
        out_specs=(any_space, any_space),
        scratch_shapes=[dma((3,))],
        compiler_params=pltpu.CompilerParams(vmem_limit_bytes=4 * 1024 * 1024),
        cost_estimate=pl.CostEstimate(flops=0, bytes_accessed=8 * ROWS * WIDTH, transcendentals=0),
        name="write_early",
    )(*(pltpu.with_memory_space_constraint(v, pltpu.VMEM) for v in (grad_image, grad_text)))
    late = pl.pallas_call(
        finish,
        out_shape=pltpu.VMEM((ROWS - EARLY * PIECE, WIDTH), jnp.float32),
        in_specs=[hbm, vmem, vmem, hbm],
        out_specs=vmem,
        scratch_shapes=[low_block, low_block, dma(()), dma((len(ENDS),)), dma((len(ENDS),))],
        compiler_params=pltpu.CompilerParams(
            collective_id=1, has_side_effects=True, vmem_limit_bytes=16 * 1024 * 1024
        ),
        cost_estimate=pl.CostEstimate(flops=ROWS * WIDTH, bytes_accessed=8 * ROWS * WIDTH, transcendentals=0),
        name="finish",
    )(
        captions,
        *(pltpu.with_memory_space_constraint(v, pltpu.VMEM) for v in (grad_text, partner_out)),
        pltpu.with_memory_space_constraint(image_out, pltpu.HBM),
    )
    text_out = pl.pallas_call(
        write_late,
        out_shape=whole,
        in_specs=[vmem, any_space],
        out_specs=any_space,
        scratch_shapes=[dma(())],
        input_output_aliases={1: 0},
        compiler_params=pltpu.CompilerParams(vmem_limit_bytes=4 * 1024 * 1024),
        cost_estimate=pl.CostEstimate(flops=0, bytes_accessed=8 * ROWS * WIDTH, transcendentals=0),
        name="write_late",
    )(pltpu.with_memory_space_constraint(late, pltpu.VMEM), text_out)
    return image_out, text_out


def solution(mesh):
    rows = P(("blk", "grp"), None)
    return jax.shard_map(
        local, mesh=mesh, in_specs=(rows, rows, P(("blk", "grp")), P(), P()), out_specs=(rows, rows), check_vma=False
    )
```
